512 devices in a mesh: gx: 16 (over y, core), gy: 32 (over x, z).
Axes of the slice: x: 4, y: 8, z: 8, core: 2. Of those that a mesh axis runs over, the one named last changes fastest.
Arguments:
- columns: float32 [262144, 512], P(('gx', 'gy')), may hold values from -6 to 6
- col_basis: float32 [262144, 128], P(('gx', 'gy')), may hold values from -0.25 to 0.25
- row_basis: float32 [262144, 128], P(('gx', 'gy')), may hold values from -0.5 to 0.5
- order_perm: int32 [512, 512], P(('gx', 'gy')), may hold values from 0 to 511, each once within a row
- near_blocks: float32 [2048, 5, 128, 128], P(('gx', 'gy')), may hold values from -0.25 to 0.25
- band_offsets: int32 [2048, 5], P(('gx', 'gy')), may hold values from -4 to 4
- transfer: float32 [8, 2, 128, 128], replicated, may hold values from -0.375 to 0.375
- coupling: float32 [9, 128, 128], replicated, may hold values from -0.5 to 0.5
Outputs:
- product: float32 [262144, 512], P(('gx', 'gy'))
The draws below stay inside these ranges and needn't reach their ends.
Inputs may be any that keep to these rules, and one draw needn't show every extreme that they name: `order_perm`: each row is a permutation of the 512 rows of its leaf.
All inputs are finite; a program needn't handle non-finite values.
Results may differ from the reference program's by a relative error of at most 0.0001.
Values sent between devices are 32-bit elements; how exact they have to be, the bound alone decides.
A program may use at most 64 MiB of HBM per device.

```python
import jax
import jax.numpy as jnp
from jax import lax

LEAF = 512
NRHS = 512
R = 128
BLK = 128
REACH = 4
NBAND = 5
LEVELS = 9
NBLK = 4
ORDER = 262144
DEVICES = 512


def place_ends(values, own_key, low, high):
    index_at = [jax.random.randint(jax.random.fold_in(own_key, axis), (), 0, length) for axis, length in enumerate(values.shape)]
    longest = values.shape.index(max(values.shape))
    neighbour = index_at[:longest] + [(index_at[longest] + 1) % values.shape[longest]] + index_at[longest + 1:]
    return values.at[tuple(index_at)].set(low).at[tuple(neighbour)].set(high)


def block_levels(key, dims, cuts, least, top_value):
    def one(dim, parts):
        steps = jax.random.uniform(jax.random.fold_in(jax.random.fold_in(key, 6), dim), (parts,), jnp.float32, least / len(cuts), top_value / len(cuts))
        return jnp.repeat(jnp.exp(steps), dims[dim] // parts).reshape((-1,) + (1,) * (len(dims) - dim - 1))

    level = one(*cuts[0])
    for cut in cuts[1:]:
        level = level * one(*cut)
    return level


def bell_draw(stream_key, shape, width, reach, split=(), held_as=jnp.bfloat16):
    entries = width * jax.random.normal(stream_key, shape, jnp.float32)
    if split:
        entries = entries * block_levels(stream_key, shape, split, -0.22, 0.18)
    return jnp.clip(entries, -reach, reach).astype(held_as)


def setup_inputs(seed: int = 0) -> dict:
    seeds = jax.random.split(jax.random.key(seed), 9)
    columns = bell_draw(seeds[0], (ORDER, NRHS), 1.0, 6.0, ((0, 512),), jnp.float32)
    col_basis = bell_draw(seeds[1], (ORDER, R), LEAF ** -0.5, 0.25, ((0, 512),), jnp.float32)
    row_basis = bell_draw(seeds[2], (ORDER, R), R ** -0.5, 0.5, ((0, 512),), jnp.float32)
    order_perm = jax.vmap(lambda own: jax.random.permutation(own, LEAF))(jax.random.split(seeds[3], DEVICES)).reshape((DEVICES, LEAF)).astype(jnp.int32)
    near_blocks = bell_draw(seeds[4], (DEVICES * NBLK, NBAND, BLK, BLK), (BLK * NBAND) ** -0.5, 0.25, ((0, 512),), jnp.float32)
    band_offsets = place_ends(jax.random.randint(seeds[5], (DEVICES * NBLK, NBAND), 0 - REACH, REACH + 1), jax.random.fold_in(seeds[5], 1), 0 - REACH, REACH).astype(jnp.int32)
    transfer = bell_draw(seeds[6], (LEVELS - 1, 2, R, R), (2 * R) ** -0.5, 0.375, (), jnp.float32)
    coupling = bell_draw(seeds[7], (LEVELS, R, R), R ** -0.5, 0.5, (), jnp.float32)
    return dict(columns=columns, col_basis=col_basis, row_basis=row_basis, order_perm=order_perm, near_blocks=near_blocks, band_offsets=band_offsets, transfer=transfer, coupling=coupling)


def near_field(padded_rows, blocks_here, offsets_here):
    rhs_cols = padded_rows.shape[1]
    column_blocks = padded_rows.reshape(-1, BLK, rhs_cols)
    block_index = jnp.arange(offsets_here.shape[0], dtype=jnp.int32)[:, None] + offsets_here + REACH
    taken = column_blocks[block_index]
    result = jnp.einsum("jbrc,jbcn->jrn", blocks_here, taken, precision=lax.Precision.HIGHEST)
    return result.reshape(-1, rhs_cols)


def reference(columns, col_basis, row_basis, order_perm, near_blocks, band_offsets, transfer, coupling):
    exact = lax.Precision.HIGHEST
    rhs_cols = columns.shape[1]
    leaves = columns.reshape(DEVICES, LEAF, rhs_cols)
    tree_cols = jnp.take_along_axis(leaves, order_perm[:, :, None], axis=1)
    skeleton = jnp.einsum("dlr,dln->drn", col_basis.reshape(DEVICES, LEAF, R), tree_cols, precision=exact)
    couples = []
    nodes = skeleton
    for level in range(LEVELS):
        pairs = nodes.reshape(-1, 2, R, rhs_cols)
        left_nodes = pairs[:, 0]
        right_nodes = pairs[:, 1]
        to_left = jnp.einsum("rk,pkn->prn", coupling[level], right_nodes, precision=exact)
        to_right = jnp.einsum("kr,pkn->prn", coupling[level], left_nodes, precision=exact)
        couples.append(jnp.stack([to_left, to_right], 1).reshape(-1, R, rhs_cols))
        if level < LEVELS - 1:
            nodes = jnp.einsum("kr,pkn->prn", transfer[level, 0], left_nodes, precision=exact) + jnp.einsum("kr,pkn->prn", transfer[level, 1], right_nodes, precision=exact)
    expand = couples[LEVELS - 1]
    for level in range(LEVELS - 2, -1, -1):
        down_left = jnp.einsum("rk,pkn->prn", transfer[level, 0], expand, precision=exact)
        down_right = jnp.einsum("rk,pkn->prn", transfer[level, 1], expand, precision=exact)
        expand = couples[level] + jnp.stack([down_left, down_right], 1).reshape(-1, R, rhs_cols)
    far = jnp.einsum("dlr,drn->dln", row_basis.reshape(DEVICES, LEAF, R), expand, precision=exact)
    margin = REACH * BLK
    padded = jnp.pad(tree_cols.reshape(ORDER, rhs_cols), ((margin, margin), (0, 0)))
    blocks_all = near_blocks.reshape(DEVICES, NBLK, NBAND, BLK, BLK)
    offsets_all = band_offsets.reshape(DEVICES, NBLK, NBAND)

    def one_leaf(inputs):
        leaf_index, blocks_here, offsets_here = inputs
        rows_here = lax.dynamic_slice_in_dim(padded, leaf_index * LEAF, LEAF + 2 * margin, 0)
        return near_field(rows_here, blocks_here, offsets_here)

    near = lax.map(one_leaf, (jnp.arange(DEVICES, dtype=jnp.int32), blocks_all, offsets_all))
    tree_out = near + far
    leaf_rows = jnp.arange(DEVICES, dtype=jnp.int32)[:, None]
    product = jnp.zeros_like(tree_out).at[leaf_rows, order_perm].set(tree_out)
    return product.reshape(ORDER, rhs_cols)
```

```python
import jax
import jax.numpy as jnp
from jax import lax
from jax.experimental import pallas as pl
from jax.experimental.pallas import tpu as pltpu
from jax.sharding import PartitionSpec as P

LEAF = 512
NRHS = 512
R = 128
BLK = 128
REACH = 4
NBAND = 5
NBLK = LEAF // BLK

NZ = 8
NX = 4
NC = 2
NY = 8

CW = 128
MESH = pl.DeviceIdType.MESH
F32 = jnp.float32
BF16 = jnp.bfloat16


def log2(n):
    return n.bit_length() - 1


def mm(a, b):
    return lax.dot_general(a, b, (((1,), (0,)), ((), ())), preferred_element_type=F32)


def split(x):
    high = x.astype(BF16)
    low = (x - high.astype(F32)).astype(BF16)
    return high, low


def lanes(parts):
    return jnp.concatenate(parts, axis=1)


def rows(parts):
    return jnp.concatenate(parts, axis=0)


def wide(x):
    return lanes(split(x))


def halves(x):
    half = x.shape[1] // 2
    return x[:, :half] + x[:, half:]


def kernel(
    x_hbm, v_hbm, u_hbm, perm_hbm, near_hbm, off_hbm, transfer_hbm, coupling_hbm, out_hbm,
    x_v, v_v, u_v, perm_v, near_v, off_s, transfer_v, coupling_v,
    up_w, down_w, coup_w, band, turned_band, near_w, far_w, turned, straight, total, out_v,
    skel, z_in, x_out, x_in, y_out, y_in, top, xr_out, xr_in, zr_out, zr_in,
    raw, perm_in,
    load_sem, store_sem,
    z_send, z_recv, x_send, x_recv, y_send, y_recv, xr_send, xr_recv, zr_send, zr_recv,
    halo_send, halo_recv, perm_send, perm_recv,
):
    nxc = NX * NC
    gx = lax.axis_index("gx")
    gy = lax.axis_index("gy")
    y, core = lax.div(gx, NC), lax.rem(gx, NC)
    xx, z = lax.div(gy, NZ), lax.rem(gy, NZ)
    along = NX * NZ
    leaves = along * NC * NY
    leaf = gx * along + gy
    xc = core * NX + xx
    levels = coupling_hbm.shape[0]
    chunks = NRHS // CW
    cz = NRHS // NZ
    cx = cz // nxc

    def z_dev(k):
        return (gx, xx * NZ + k)

    def x_dev(k):
        return (y * NC + lax.div(k, NX), lax.rem(k, NX) * NZ + z)

    def y_dev(k):
        return (k * NC + core, gy)

    def leaf_dev(k):
        return (lax.div(k, along), lax.rem(k, along))

    right = leaf_dev(lax.rem(leaf + 1, leaves))
    left = leaf_dev(lax.rem(leaf + leaves - 1, leaves))

    def remote(src, dst, send, recv, dev):
        return pltpu.make_async_remote_copy(
            src_ref=src, dst_ref=dst, send_sem=send, recv_sem=recv, device_id=dev, device_id_type=MESH
        )

    loads = [
        pltpu.make_async_copy(src, dst, load_sem.at[i])
        for i, (src, dst) in enumerate(
            (
                (perm_hbm, perm_v),
                (v_hbm, v_v),
                (x_hbm, x_v),
                (transfer_hbm, transfer_v),
                (coupling_hbm, coupling_v),
                (near_hbm, near_v),
                (u_hbm, u_v),
                (off_hbm, off_s),
            )
        )
    ]
    for load in loads:
        load.start()

    barrier = pltpu.get_barrier_semaphore()
    greeted = (
        [z_dev(lax.rem(z + k, NZ)) for k in range(1, NZ)]
        + [x_dev(lax.rem(xc + k, nxc)) for k in range(1, nxc)]
        + [y_dev(lax.rem(y + k, NY)) for k in range(1, NY)]
        + [left, right]
    )
    for dev in greeted:
        pl.semaphore_signal(barrier, inc=1, device_id=dev, device_id_type=MESH)
    pl.semaphore_wait(barrier, len(greeted))

    def halo(side, chunk):
        return remote(
            x_hbm.at[:, pl.ds(chunk * CW, CW)],
            raw.at[side, chunk],
            halo_send.at[side, chunk],
            halo_recv.at[side, chunk],
            (right, left)[side],
        )

    def halo_perm(side):
        return remote(
            perm_hbm, perm_in.at[side], perm_send.at[side], perm_recv.at[side], (right, left)[side]
        )

    for side in range(2):
        halo_perm(side).start()
        halo(side, 0).start()

    loads[0].wait()
    perm_row = perm_v[...]
    hit = lax.broadcasted_iota(jnp.int32, (LEAF, LEAF), 0) == perm_row
    turned[...] = jnp.where(hit, 1.0, 0.0).astype(BF16)
    loads[1].wait()
    basis = mm(turned[...], wide(v_v[...]))
    basis_t = basis.T.astype(BF16)
    loads[2].wait()
    for c in range(chunks):
        x_wide = wide(x_v[:, c * CW : (c + 1) * CW])
        s = mm(basis_t, x_wide)
        s = halves(s)
        s = s[:R] + s[R:]
        skel[c * CW : (c + 1) * CW, :] = s.T

    def z_copy(k):
        to = lax.rem(z + k, NZ)
        return remote(
            skel.at[pl.ds(to * cz, cz), :], z_in.at[z], z_send.at[k], z_recv.at[k], z_dev(to)
        )

    for k in range(1, NZ):
        z_copy(k).start()
    z_in[z] = skel[pl.ds(z * cz, cz), :]
    for chunk in range(1, chunks):
        for side in range(2):
            halo(side, chunk).start()

    loads[3].wait()
    loads[4].wait()

    def prepare(m, _):
        up_w[m] = wide(transfer_v[m])
        w = transfer_v[m]
        w = wide(lanes([w[:R].T, w[R:].T]))
        down_w[m] = rows([w, w])
        return 0

    lax.fori_loop(0, levels - 1, prepare, 0)

    def prepare_coupling(m, _):
        c = coupling_v[m]
        w = wide(c.T)
        coup_w[m, 0] = rows([w, w])
        w = wide(c)
        coup_w[m, 1] = rows([w, w])
        return 0

    lax.fori_loop(0, levels, prepare_coupling, 0)

    loads[5].wait()
    loads[7].wait()
    band[...] = jnp.zeros(band.shape, BF16)

    def fill_band(b, _):
        at_rows = pl.ds(pl.multiple_of(b * BLK, BLK), BLK)
        for offset in range(2 * REACH + 1):
            block = jnp.zeros((BLK, BLK), F32)
            for j in range(NBAND):
                here = jnp.where(off_s[b, j] == offset - REACH, 1.0, 0.0).astype(F32)
                block = block + near_v[b, j] * here
            at_lanes = pl.ds(pl.multiple_of((b + offset) * BLK, BLK), BLK)
            high, low = split(block)
            band[0, at_rows, at_lanes] = high
            band[1, at_rows, at_lanes] = low
        return 0

    lax.fori_loop(0, NBLK, fill_band, 0)

    def turn_band(i, _):
        at_lanes = pl.ds(pl.multiple_of(i * 2 * BLK, 2 * BLK), 2 * BLK)
        for part in range(2):
            turned_band[part * LEAF : (part + 1) * LEAF, at_lanes] = mm(
                turned[...], band[part, :, at_lanes]
            ).astype(BF16)
        return 0

    lax.fori_loop(0, 3 * LEAF // (2 * BLK), turn_band, 0)

    loads[6].wait()
    spread = mm(turned[...], wide(u_v[...])).astype(BF16)
    far_w[0:LEAF, :] = spread[:, :R]
    far_w[LEAF : 2 * LEAF, :] = spread[:, R:]

    def one_hot(perm):
        column = jnp.broadcast_to(perm.astype(F32), (R, LEAF)).T
        lane = lax.broadcasted_iota(jnp.int32, (LEAF, R), 1).astype(F32)
        for i in range(LEAF // R):
            straight[:, i * R : (i + 1) * R] = jnp.where(
                column == lane + float(i * R), 1.0, 0.0
            ).astype(BF16)

    def fold(place, perm, factor):
        one_hot(perm)

        def fold_rows(i, _):
            at_rows = pl.ds(pl.multiple_of(i * 2 * BLK, 2 * BLK), 2 * BLK)
            got = mm(turned_band[at_rows, place * LEAF : (place + 1) * LEAF], straight[...])
            near_w[place, at_rows, :] = (got * factor).astype(BF16)
            return 0

        lax.fori_loop(0, 2 * LEAF // (2 * BLK), fold_rows, 0)

    def near_part(place, x):
        r = halves(mm(near_w[place], wide(x)))
        return r[:LEAF] + r[LEAF:]

    def up(m, nodes):
        n = len(nodes) // 2 * nodes[0].shape[0]
        lh, ll = split(rows(nodes[0::2]))
        rh, rl = split(rows(nodes[1::2]))
        to_left = halves(mm(lanes([rh, rl]), coup_w[m, 0]))
        to_right = halves(mm(lanes([lh, ll]), coup_w[m, 1]))
        if m == levels - 1:
            return (to_left, to_right), None
        both = rows([lanes([lh, rh]), lanes([ll, rl])])
        parent = halves(mm(both, up_w[m]))
        parent = parent[:n] + parent[n:]
        return (to_left, to_right), cut(parent, len(nodes) // 2)

    def cut(x, parts):
        each = x.shape[0] // parts
        return [x[i * each : (i + 1) * each] for i in range(parts)]

    def down(m, coup, nodes):
        d = halves(mm(wide(rows(nodes)), down_w[m]))
        lefts = cut(coup[0] + d[:, :R], len(nodes))
        rights = cut(coup[1] + d[:, R:], len(nodes))
        return [node for pair in zip(lefts, rights) for node in pair]

    lz, lx, ly = log2(NZ), log2(nxc), log2(NY)
    coups = [None] * levels
    for k in range(1, NZ):
        z_copy(k).wait_recv()
    nodes = [z_in[k] for k in range(NZ)]
    for m in range(lz):
        coups[m], nodes = up(m, nodes)
    x_out[...] = nodes[0]

    def x_copy(k):
        to = lax.rem(xc + k, nxc)
        return remote(
            x_out.at[pl.ds(to * cx, cx), :], x_in.at[xc], x_send.at[k], x_recv.at[k], x_dev(to)
        )

    for k in range(1, nxc):
        x_copy(k).start()
    x_in[xc] = x_out[pl.ds(xc * cx, cx), :]
    fold(1, perm_row, 1.0)
    for k in range(1, nxc):
        x_copy(k).wait_recv()
    nodes = [x_in[k] for k in range(nxc)]
    for m in range(lz, lz + lx):
        coups[m], nodes = up(m, nodes)
    y_out[...] = nodes[0]

    def y_copy(k):
        to = lax.rem(y + k, NY)
        return remote(y_out, y_in.at[y], y_send.at[k], y_recv.at[k], y_dev(to))

    for k in range(1, NY):
        y_copy(k).start()
    y_in[y] = y_out[...]
    halo_perm(0).wait_recv()
    fold(0, perm_in[0], jnp.where(leaf > 0, 1.0, 0.0).astype(F32))
    for k in range(1, NY):
        y_copy(k).wait_recv()
    nodes = [y_in[k] for k in range(NY)]
    for m in range(lz + lx, levels):
        coups[m], nodes = up(m, nodes)
    nodes = [coups[levels - 1][0], coups[levels - 1][1]]
    for m in range(levels - 2, lz + lx - 1, -1):
        nodes = down(m, coups[m], nodes)
    for k in range(NY):
        top[k] = nodes[k]
    nodes = [top[y]]
    for m in range(lz + lx - 1, lz - 1, -1):
        nodes = down(m, coups[m], nodes)
    for k in range(nxc):
        xr_out[k] = nodes[k]

    def xr_copy(k):
        to = lax.rem(xc + k, nxc)
        return remote(xr_out.at[to], xr_in.at[xc], xr_send.at[k], xr_recv.at[k], x_dev(to))

    for k in range(1, nxc):
        xr_copy(k).start()
    xr_in[xc] = xr_out[xc]
    halo_perm(1).wait_recv()
    fold(2, perm_in[1], jnp.where(leaf < leaves - 1, 1.0, 0.0).astype(F32))
    for k in range(1, nxc):
        xr_copy(k).wait_recv()
    nodes = [rows([xr_in[k] for k in range(nxc)])]
    for m in range(lz - 1, -1, -1):
        nodes = down(m, coups[m], nodes)
    for k in range(NZ):
        zr_out[k] = nodes[k]

    def zr_copy(k):
        to = lax.rem(z + k, NZ)
        return remote(zr_out.at[to], zr_in.at[z], zr_send.at[k], zr_recv.at[k], z_dev(to))

    for k in range(1, NZ):
        zr_copy(k).start()
    zr_in[z] = zr_out[z]

    for c in range(chunks):
        total[c] = near_part(1, x_v[:, c * CW : (c + 1) * CW])
    for c in range(chunks):
        for side in range(2):
            halo(side, c).wait_recv()
            total[c] = total[c] + near_part(2 * side, raw[side, c])

    for k in range(1, NZ):
        zr_copy(k).wait_recv()
    for c in range(chunks):
        each = CW // cz if CW >= cz else 1
        if CW >= cz:
            e = rows([zr_in[c * each + i] for i in range(each)])
        else:
            e = zr_in[c * CW // cz, c * CW % cz : c * CW % cz + CW]
        r = halves(mm(far_w[...], wide(e.T)))
        out_v[c] = total[c] + r[:LEAF] + r[LEAF:]
        pltpu.make_async_copy(
            out_v.at[c], out_hbm.at[:, pl.ds(c * CW, CW)], store_sem.at[c]
        ).start()
    for c in range(chunks):
        pltpu.make_async_copy(
            out_v.at[c], out_hbm.at[:, pl.ds(c * CW, CW)], store_sem.at[c]
        ).wait()

    for k in range(1, NZ):
        z_copy(k).wait_send()
        zr_copy(k).wait_send()
    for k in range(1, nxc):
        x_copy(k).wait_send()
        xr_copy(k).wait_send()
    for k in range(1, NY):
        y_copy(k).wait_send()
    for side in range(2):
        halo_perm(side).wait_send()
        for chunk in range(chunks):
            halo(side, chunk).wait_send()


def per_device(
    columns, col_basis, row_basis, order_perm, near_blocks, band_offsets, transfer, coupling
):
    nxc = NX * NC
    levels = coupling.shape[0]
    chunks = NRHS // CW
    cz = NRHS // NZ
    cx = cz // nxc
    transfer = transfer.reshape(levels - 1, 2 * R, R)
    vmem = pltpu.VMEM
    dma = pltpu.SemaphoreType.DMA
    return pl.pallas_call(
        kernel,
        out_shape=jax.ShapeDtypeStruct((LEAF, NRHS), F32),
        in_specs=[pl.BlockSpec(memory_space=pl.ANY)] * 8,
        out_specs=pl.BlockSpec(memory_space=pl.ANY),
        scratch_shapes=[
            vmem((LEAF, NRHS), F32),
            vmem((LEAF, R), F32),
            vmem((LEAF, R), F32),
            vmem((1, LEAF), jnp.int32),
            vmem((NBLK, NBAND, BLK, BLK), F32),
            pltpu.SMEM((NBLK, NBAND), jnp.int32),
            vmem((levels - 1, 2 * R, R), F32),
            vmem((levels, R, R), F32),
            vmem((levels - 1, 2 * R, 2 * R), BF16),
            vmem((levels - 1, 2 * R, 4 * R), BF16),
            vmem((levels, 2, 2 * R, 2 * R), BF16),
            vmem((2, LEAF, 3 * LEAF), BF16),
            vmem((2 * LEAF, 3 * LEAF), BF16),
            vmem((3, 2 * LEAF, LEAF), BF16),
            vmem((2 * LEAF, R), BF16),
            vmem((LEAF, LEAF), BF16),
            vmem((LEAF, LEAF), BF16),
            vmem((chunks, LEAF, CW), F32),
            vmem((chunks, LEAF, CW), F32),
            vmem((NRHS, R), F32),
            vmem((NZ, cz, R), F32),
            vmem((cz, R), F32),
            vmem((nxc, cx, R), F32),
            vmem((cx, R), F32),
            vmem((NY, cx, R), F32),
            vmem((NY, cx, R), F32),
            vmem((nxc, cx, R), F32),
            vmem((nxc, cx, R), F32),
            vmem((NZ, cz, R), F32),
            vmem((NZ, cz, R), F32),
            vmem((2, chunks, LEAF, CW), F32),
            vmem((2, 1, LEAF), jnp.int32),
            dma((8,)),
            dma((chunks,)),
            dma((NZ,)),
            dma((NZ,)),
            dma((nxc,)),
            dma((nxc,)),
            dma((NY,)),
            dma((NY,)),
            dma((nxc,)),
            dma((nxc,)),
            dma((NZ,)),
            dma((NZ,)),
            dma((2, chunks)),
            dma((2, chunks)),
            dma((2,)),
            dma((2,)),
        ],
        compiler_params=pltpu.CompilerParams(
            collective_id=0, has_side_effects=True, vmem_limit_bytes=58 * 1024 * 1024
        ),
    )(
        columns, col_basis, row_basis, order_perm, near_blocks, band_offsets, transfer, coupling
    )


def solution(mesh):
    placed = (
        P(("gx", "gy"), None),
        P(("gx", "gy"), None),
        P(("gx", "gy"), None),
        P(("gx", "gy"), None),
        P(("gx", "gy"), None, None, None),
        P(("gx", "gy"), None),
        P(),
        P(),
    )
    return jax.shard_map(
        per_device, mesh=mesh, in_specs=placed, out_specs=P(("gx", "gy"), None), check_vma=False
    )
```

```python
import jax
import jax.numpy as jnp
from jax import lax
from jax.experimental import pallas as pl
from jax.experimental.pallas import tpu as pltpu
from jax.sharding import PartitionSpec as P

LEAF = 512
NRHS = 512
R = 128
BLK = 128
REACH = 4
NBAND = 5
NBLK = LEAF // BLK

NZ = 8
NX = 4
NC = 2
NY = 8

CW = 128
MESH = pl.DeviceIdType.MESH
F32 = jnp.float32
BF16 = jnp.bfloat16


def log2(n):
    return n.bit_length() - 1


def mm(a, b):
    return lax.dot_general(a, b, (((1,), (0,)), ((), ())), preferred_element_type=F32)


def split(x):
    high = x.astype(BF16)
    low = (x - high.astype(F32)).astype(BF16)
    return high, low


def lanes(parts):
    return jnp.concatenate(parts, axis=1)


def rows(parts):
    return jnp.concatenate(parts, axis=0)


def wide(x):
    return lanes(split(x))


def halves(x):
    half = x.shape[1] // 2
    return x[:, :half] + x[:, half:]


def kernel(
    x_hbm, v_hbm, u_hbm, perm_hbm, near_hbm, off_hbm, transfer_hbm, coupling_hbm, product,
    x_v, v_v, u_v, perm_v, near_v, off_s, transfer_v, coupling_v,
    up_w, down_w, coup_w, band, turned_band, near_w, far_w, turned, straight, total,
    skel, up_in, y_out, y_in, top, down_out, down_in,
    raw, perm_in,
    load_sem,
    up_send, up_recv, y_send, y_recv, down_send, down_recv,
    halo_send, halo_recv, perm_send, perm_recv,
):
    gx = lax.axis_index("gx")
    gy = lax.axis_index("gy")
    y, core = lax.div(gx, NC), lax.rem(gx, NC)
    along = NX * NZ
    team = along * NC
    leaves = team * NY
    leaf = gx * along + gy
    place = core * along + gy
    levels = coupling_hbm.shape[0]
    chunks = NRHS // CW
    share = NRHS // team

    def team_dev(k):
        return (y * NC + lax.div(k, along), lax.rem(k, along))

    def y_dev(k):
        return (k * NC + core, gy)

    def leaf_dev(k):
        return (lax.div(k, along), lax.rem(k, along))

    right = leaf_dev(lax.rem(leaf + 1, leaves))
    left = leaf_dev(lax.rem(leaf + leaves - 1, leaves))

    def remote(src, dst, send, recv, dev):
        return pltpu.make_async_remote_copy(
            src_ref=src, dst_ref=dst, send_sem=send, recv_sem=recv, device_id=dev, device_id_type=MESH
        )

    loads = [
        pltpu.make_async_copy(src, dst, load_sem.at[i])
        for i, (src, dst) in enumerate(
            (
                (perm_hbm, perm_v),
                (v_hbm, v_v),
                (x_hbm, x_v),
                (transfer_hbm, transfer_v),
                (coupling_hbm, coupling_v),
                (near_hbm, near_v),
                (u_hbm, u_v),
                (off_hbm, off_s),
            )
        )
    ]
    for load in loads:
        load.start()

    barrier = pltpu.get_barrier_semaphore()
    greeted = (
        [y_dev(lax.rem(y + k, NY)) for k in range(1, NY)]
        + [left, right]
    )
    for dev in greeted:
        pl.semaphore_signal(barrier, inc=1, device_id=dev, device_id_type=MESH)

    def greet(k, _):
        dev = team_dev(lax.rem(place + k, team))
        pl.semaphore_signal(barrier, inc=1, device_id=dev, device_id_type=MESH)
        return 0

    lax.fori_loop(1, team, greet, 0)
    pl.semaphore_wait(barrier, len(greeted) + team - 1)

    def halo(side, chunk):
        return remote(
            x_hbm.at[:, pl.ds(chunk * CW, CW)],
            raw.at[side, chunk],
            halo_send.at[side, chunk],
            halo_recv.at[side, chunk],
            (right, left)[side],
        )

    def halo_perm(side):
        return remote(
            perm_hbm, perm_in.at[side], perm_send.at[side], perm_recv.at[side], (right, left)[side]
        )

    def send_halo(*which):
        for chunk in which:
            for side in range(2):
                halo(side, chunk).start()

    for side in range(2):
        halo_perm(side).start()
    send_halo(0)

    loads[0].wait()
    perm_row = perm_v[...]
    hit = lax.broadcasted_iota(jnp.int32, (LEAF, LEAF), 0) == perm_row
    turned[...] = jnp.where(hit, 1.0, 0.0).astype(BF16)
    loads[1].wait()
    basis = mm(turned[...], wide(v_v[...]))
    basis_t = basis.T.astype(BF16)
    loads[2].wait()
    for c in range(chunks):
        x_wide = wide(x_v[:, c * CW : (c + 1) * CW])
        s = mm(basis_t, x_wide)
        s = halves(s)
        s = s[:R] + s[R:]
        skel[c * CW : (c + 1) * CW, :] = s.T

    def up_start(k, _):
        to = lax.rem(place + k, team)
        remote(
            skel.at[pl.ds(pl.multiple_of(to * share, share), share), :],
            up_in.at[place], up_send, up_recv, team_dev(to),
        ).start()
        return 0

    def all_but_one(buf, sem, n):
        return pltpu.make_async_copy(buf.at[pl.ds(0, n - 1)], buf.at[pl.ds(0, n - 1)], sem)

    lax.fori_loop(1, team, up_start, 0)
    send_halo(1)
    up_in[place] = skel[pl.ds(pl.multiple_of(place * share, share), share), :]

    loads[3].wait()
    loads[4].wait()

    def prepare(m, _):
        up_w[m] = wide(transfer_v[m])
        w = transfer_v[m]
        w = wide(lanes([w[:R].T, w[R:].T]))
        down_w[m] = rows([w, w])
        return 0

    lax.fori_loop(0, levels - 1, prepare, 0)

    def prepare_coupling(m, _):
        c = coupling_v[m]
        w = wide(c.T)
        coup_w[m, 0] = rows([w, w])
        w = wide(c)
        coup_w[m, 1] = rows([w, w])
        return 0

    lax.fori_loop(0, levels, prepare_coupling, 0)

    loads[5].wait()
    loads[7].wait()
    band[...] = jnp.zeros(band.shape, BF16)

    def fill_band(b, _):
        at_rows = pl.ds(pl.multiple_of(b * BLK, BLK), BLK)
        for offset in range(2 * REACH + 1):
            block = jnp.zeros((BLK, BLK), F32)
            for j in range(NBAND):
                here = jnp.where(off_s[b, j] == offset - REACH, 1.0, 0.0).astype(F32)
                block = block + near_v[b, j] * here
            at_lanes = pl.ds(pl.multiple_of((b + offset) * BLK, BLK), BLK)
            high, low = split(block)
            band[0, at_rows, at_lanes] = high
            band[1, at_rows, at_lanes] = low
        return 0

    lax.fori_loop(0, NBLK, fill_band, 0)

    def turn_band(i, _):
        at_lanes = pl.ds(pl.multiple_of(i * 2 * BLK, 2 * BLK), 2 * BLK)
        for part in range(2):
            turned_band[part * LEAF : (part + 1) * LEAF, at_lanes] = mm(
                turned[...], band[part, :, at_lanes]
            ).astype(BF16)
        return 0

    lax.fori_loop(0, 3 * LEAF // (2 * BLK), turn_band, 0)

    loads[6].wait()
    spread = mm(turned[...], wide(u_v[...])).astype(BF16)
    far_w[0:LEAF, :] = spread[:, :R]
    far_w[LEAF : 2 * LEAF, :] = spread[:, R:]

    def one_hot(perm):
        column = jnp.broadcast_to(perm.astype(F32), (R, LEAF)).T
        lane = lax.broadcasted_iota(jnp.int32, (LEAF, R), 1).astype(F32)
        for i in range(LEAF // R):
            straight[:, i * R : (i + 1) * R] = jnp.where(
                column == lane + float(i * R), 1.0, 0.0
            ).astype(BF16)

    def fold(which, perm, factor):
        one_hot(perm)

        def fold_rows(i, _):
            at_rows = pl.ds(pl.multiple_of(i * 2 * BLK, 2 * BLK), 2 * BLK)
            got = mm(turned_band[at_rows, which * LEAF : (which + 1) * LEAF], straight[...])
            near_w[which, at_rows, :] = (got * factor).astype(BF16)
            return 0

        lax.fori_loop(0, 2 * LEAF // (2 * BLK), fold_rows, 0)

    def near_part(which, x):
        r = halves(mm(near_w[which], wide(x)))
        return r[:LEAF] + r[LEAF:]

    def up(m, nodes):
        n = len(nodes) // 2 * nodes[0].shape[0]
        lh, ll = split(rows(nodes[0::2]))
        rh, rl = split(rows(nodes[1::2]))
        to_left = halves(mm(lanes([rh, rl]), coup_w[m, 0]))
        to_right = halves(mm(lanes([lh, ll]), coup_w[m, 1]))
        if m == levels - 1:
            return (to_left, to_right), None
        both = rows([lanes([lh, rh]), lanes([ll, rl])])
        parent = halves(mm(both, up_w[m]))
        parent = parent[:n] + parent[n:]
        return (to_left, to_right), cut(parent, len(nodes) // 2)

    def cut(x, parts):
        each = x.shape[0] // parts
        return [x[i * each : (i + 1) * each] for i in range(parts)]

    def down(m, coup, nodes):
        d = halves(mm(wide(rows(nodes)), down_w[m]))
        lefts = cut(coup[0] + d[:, :R], len(nodes))
        rights = cut(coup[1] + d[:, R:], len(nodes))
        return [node for pair in zip(lefts, rights) for node in pair]

    within = log2(team)
    coups = [None] * levels
    all_but_one(up_in, up_recv, team).wait()
    send_halo(2, 3)
    nodes = [up_in[k] for k in range(team)]
    for m in range(within):
        coups[m], nodes = up(m, nodes)
    y_out[...] = nodes[0]
    for k in range(1, NY):
        to = lax.rem(y + k, NY)
        remote(y_out, y_in.at[y], y_send, y_recv, y_dev(to)).start()
    y_in[y] = y_out[...]
    fold(1, perm_row, 1.0)
    all_but_one(y_in, y_recv, NY).wait()
    nodes = [y_in[k] for k in range(NY)]
    for m in range(within, levels):
        coups[m], nodes = up(m, nodes)
    nodes = [coups[levels - 1][0], coups[levels - 1][1]]
    for m in range(levels - 2, within - 1, -1):
        nodes = down(m, coups[m], nodes)
    for k in range(NY):
        top[k] = nodes[k]
    nodes = [top[y]]
    for m in range(within - 1, -1, -1):
        nodes = down(m, coups[m], nodes)
    for k in range(team):
        down_out[k] = nodes[k]

    def down_start(k, _):
        to = lax.rem(place + k, team)
        remote(down_out.at[to], down_in.at[place], down_send, down_recv, team_dev(to)).start()
        return 0

    lax.fori_loop(1, team, down_start, 0)
    down_in[place] = down_out[place]

    for side in range(2):
        halo_perm(side).wait_recv()
    fold(0, perm_in[0], jnp.where(leaf > 0, 1.0, 0.0).astype(F32))
    fold(2, perm_in[1], jnp.where(leaf < leaves - 1, 1.0, 0.0).astype(F32))
    for c in range(chunks):
        total[c] = near_part(1, x_v[:, c * CW : (c + 1) * CW])
    for c in range(chunks):
        for side in range(2):
            halo(side, c).wait_recv()
            total[c] = total[c] + near_part(2 * side, raw[side, c])

    all_but_one(down_in, down_recv, team).wait()
    expanded = down_in[...].reshape(NRHS, R)
    for c in range(chunks):
        r = halves(mm(far_w[...], wide(expanded[c * CW : (c + 1) * CW].T)))
        product[:, c * CW : (c + 1) * CW] = total[c] + r[:LEAF] + r[LEAF:]
    all_but_one(up_in, up_send, team).wait()
    all_but_one(down_in, down_send, team).wait()
    all_but_one(y_in, y_send, NY).wait()
    for side in range(2):
        halo_perm(side).wait_send()
        for chunk in range(chunks):
            halo(side, chunk).wait_send()


def per_device(
    columns, col_basis, row_basis, order_perm, near_blocks, band_offsets, transfer, coupling
):
    levels = coupling.shape[0]
    chunks = NRHS // CW
    team = NX * NC * NZ
    share = NRHS // team
    transfer = transfer.reshape(levels - 1, 2 * R, R)
    vmem = pltpu.VMEM
    dma = pltpu.SemaphoreType.DMA
    return pl.pallas_call(
        kernel,
        out_shape=vmem((LEAF, NRHS), F32),
        in_specs=[pl.BlockSpec(memory_space=pl.ANY)] * 8,
        out_specs=pl.BlockSpec(memory_space=pltpu.VMEM),
        scratch_shapes=[
            vmem((LEAF, NRHS), F32),
            vmem((LEAF, R), F32),
            vmem((LEAF, R), F32),
            vmem((1, LEAF), jnp.int32),
            vmem((NBLK, NBAND, BLK, BLK), F32),
            pltpu.SMEM((NBLK, NBAND), jnp.int32),
            vmem((levels - 1, 2 * R, R), F32),
            vmem((levels, R, R), F32),
            vmem((levels - 1, 2 * R, 2 * R), BF16),
            vmem((levels - 1, 2 * R, 4 * R), BF16),
            vmem((levels, 2, 2 * R, 2 * R), BF16),
            vmem((2, LEAF, 3 * LEAF), BF16),
            vmem((2 * LEAF, 3 * LEAF), BF16),
            vmem((3, 2 * LEAF, LEAF), BF16),
            vmem((2 * LEAF, R), BF16),
            vmem((LEAF, LEAF), BF16),
            vmem((LEAF, LEAF), BF16),
            vmem((chunks, LEAF, CW), F32),
            vmem((NRHS, R), F32),
            vmem((team, share, R), F32),
            vmem((share, R), F32),
            vmem((NY, share, R), F32),
            vmem((NY, share, R), F32),
            vmem((team, share, R), F32),
            vmem((team, share, R), F32),
            vmem((2, chunks, LEAF, CW), F32),
            vmem((2, 1, LEAF), jnp.int32),
            dma((8,)),
            dma,
            dma,
            dma,
            dma,
            dma,
            dma,
            dma((2, chunks)),
            dma((2, chunks)),
            dma((2,)),
            dma((2,)),
        ],
        compiler_params=pltpu.CompilerParams(
            collective_id=0, has_side_effects=True, vmem_limit_bytes=58 * 1024 * 1024
        ),
    )(
        columns, col_basis, row_basis, order_perm, near_blocks, band_offsets, transfer, coupling
    )


def solution(mesh):
    placed = (
        P(("gx", "gy"), None),
        P(("gx", "gy"), None),
        P(("gx", "gy"), None),
        P(("gx", "gy"), None),
        P(("gx", "gy"), None, None, None),
        P(("gx", "gy"), None),
        P(),
        P(),
    )
    return jax.shard_map(
        per_device, mesh=mesh, in_specs=placed, out_specs=P(("gx", "gy"), None), check_vma=False
    )
```

```python
import jax
import jax.numpy as jnp
from jax import lax
from jax.experimental import pallas as pl
from jax.experimental.pallas import tpu as pltpu
from jax.sharding import PartitionSpec as P

LEAF = 512
NRHS = 512
R = 128
BLK = 128
REACH = 4
NBAND = 5
NBLK = LEAF // BLK

NZ = 8
NX = 4
NC = 2
NY = 8

CW = 128
MESH = pl.DeviceIdType.MESH
F32 = jnp.float32
BF16 = jnp.bfloat16


def log2(n):
    return n.bit_length() - 1


def mm(a, b):
    return lax.dot_general(a, b, (((1,), (0,)), ((), ())), preferred_element_type=F32)


def split(x):
    high = x.astype(BF16)
    low = (x - high.astype(F32)).astype(BF16)
    return high, low


def lanes(parts):
    return jnp.concatenate(parts, axis=1)


def rows(parts):
    return jnp.concatenate(parts, axis=0)


def wide(x):
    return lanes(split(x))


def halves(x):
    half = x.shape[1] // 2
    return x[:, :half] + x[:, half:]


def kernel(
    x_hbm, v_hbm, u_hbm, perm_hbm, near_hbm, off_hbm, transfer_hbm, coupling_hbm, product,
    x_v, v_v, u_v, perm_v, near_v, off_s, transfer_v, coupling_v,
    up_w, down_w, coup_w, band, turned_band, near_w, far_w, turned, straight, total,
    skel, up_in, y_out, y_in, top, down_out, down_in,
    raw, perm_in,
    load_sem,
    up_send, up_recv, y_send, y_recv, down_send, down_recv,
    halo_send, halo_recv, perm_send, perm_recv,
):
    gx = lax.axis_index("gx")
    gy = lax.axis_index("gy")
    y, core = lax.div(gx, NC), lax.rem(gx, NC)
    along = NX * NZ
    team = along * NC
    leaves = team * NY
    leaf = gx * along + gy
    place = core * along + gy
    levels = coupling_hbm.shape[0]
    chunks = NRHS // CW
    share = NRHS // team

    def team_dev(k):
        return (y * NC + lax.div(k, along), lax.rem(k, along))

    def y_dev(k):
        return (k * NC + core, gy)

    def leaf_dev(k):
        return (lax.div(k, along), lax.rem(k, along))

    right = leaf_dev(lax.rem(leaf + 1, leaves))
    left = leaf_dev(lax.rem(leaf + leaves - 1, leaves))

    def remote(src, dst, send, recv, dev):
        return pltpu.make_async_remote_copy(
            src_ref=src, dst_ref=dst, send_sem=send, recv_sem=recv, device_id=dev, device_id_type=MESH
        )

    loads = [
        pltpu.make_async_copy(src, dst, load_sem.at[i])
        for i, (src, dst) in enumerate(
            (
                (perm_hbm, perm_v),
                (v_hbm, v_v),
                (x_hbm, x_v),
                (transfer_hbm, transfer_v),
                (coupling_hbm, coupling_v),
                (near_hbm, near_v),
                (u_hbm, u_v),
                (off_hbm, off_s),
            )
        )
    ]
    for load in loads:
        load.start()

    barrier = pltpu.get_barrier_semaphore()
    greeted = (
        [y_dev(lax.rem(y + k, NY)) for k in range(1, NY)]
        + [left, right]
    )
    for dev in greeted:
        pl.semaphore_signal(barrier, inc=1, device_id=dev, device_id_type=MESH)

    def greet(k, _):
        dev = team_dev(lax.rem(place + k, team))
        pl.semaphore_signal(barrier, inc=1, device_id=dev, device_id_type=MESH)
        return 0

    lax.fori_loop(1, team, greet, 0)
    pl.semaphore_wait(barrier, len(greeted) + team - 1)

    def halo(side, chunk):
        return remote(
            x_hbm.at[:, pl.ds(chunk * CW, CW)],
            raw.at[side, chunk],
            halo_send.at[side, chunk],
            halo_recv.at[side, chunk],
            (right, left)[side],
        )

    def halo_perm(side):
        return remote(
            perm_hbm, perm_in.at[side], perm_send.at[side], perm_recv.at[side], (right, left)[side]
        )

    def send_halo(*which):
        for chunk in which:
            for side in range(2):
                halo(side, chunk).start()

    for side in range(2):
        halo_perm(side).start()
    send_halo(0)

    loads[0].wait()
    perm_row = perm_v[...]
    hit = lax.broadcasted_iota(jnp.int32, (LEAF, LEAF), 0) == perm_row
    turned[...] = jnp.where(hit, 1.0, 0.0).astype(BF16)
    loads[1].wait()
    basis = mm(turned[...], wide(v_v[...]))
    basis_t = basis.T.astype(BF16)
    loads[2].wait()
    for c in range(chunks):
        x_wide = wide(x_v[:, c * CW : (c + 1) * CW])
        s = mm(basis_t, x_wide)
        s = halves(s)
        s = s[:R] + s[R:]
        skel[c * CW : (c + 1) * CW, :] = s.T

    def up_start(k, _):
        to = lax.rem(place + k, team)
        remote(
            skel.at[pl.ds(pl.multiple_of(to * share, share), share), :],
            up_in.at[place], up_send, up_recv, team_dev(to),
        ).start()
        return 0

    def all_but_one(buf, sem, n):
        return pltpu.make_async_copy(buf.at[pl.ds(0, n - 1)], buf.at[pl.ds(0, n - 1)], sem)

    lax.fori_loop(1, team, up_start, 0)
    send_halo(1, 2)
    up_in[place] = skel[pl.ds(pl.multiple_of(place * share, share), share), :]

    loads[3].wait()
    loads[4].wait()

    def prepare(m, _):
        up_w[m] = wide(transfer_v[m])
        w = transfer_v[m]
        w = wide(lanes([w[:R].T, w[R:].T]))
        down_w[m] = rows([w, w])
        return 0

    lax.fori_loop(0, levels - 1, prepare, 0)

    def prepare_coupling(m, _):
        c = coupling_v[m]
        w = wide(c.T)
        coup_w[m, 0] = rows([w, w])
        w = wide(c)
        coup_w[m, 1] = rows([w, w])
        return 0

    lax.fori_loop(0, levels, prepare_coupling, 0)

    loads[5].wait()
    loads[7].wait()
    band[...] = jnp.zeros(band.shape, BF16)

    def fill_band(b, _):
        at_rows = pl.ds(pl.multiple_of(b * BLK, BLK), BLK)
        for offset in range(2 * REACH + 1):
            block = jnp.zeros((BLK, BLK), F32)
            for j in range(NBAND):
                here = jnp.where(off_s[b, j] == offset - REACH, 1.0, 0.0).astype(F32)
                block = block + near_v[b, j] * here
            at_lanes = pl.ds(pl.multiple_of((b + offset) * BLK, BLK), BLK)
            high, low = split(block)
            band[0, at_rows, at_lanes] = high
            band[1, at_rows, at_lanes] = low
        return 0

    lax.fori_loop(0, NBLK, fill_band, 0)

    def turn_band(i, _):
        at_lanes = pl.ds(pl.multiple_of(i * 2 * BLK, 2 * BLK), 2 * BLK)
        for part in range(2):
            turned_band[part * LEAF : (part + 1) * LEAF, at_lanes] = mm(
                turned[...], band[part, :, at_lanes]
            ).astype(BF16)
        return 0

    lax.fori_loop(0, 3 * LEAF // (2 * BLK), turn_band, 0)

    loads[6].wait()
    far_w[...] = mm(turned[...], wide(u_v[...])).astype(BF16)

    def one_hot(perm):
        column = jnp.broadcast_to(perm.astype(F32), (R, LEAF)).T
        lane = lax.broadcasted_iota(jnp.int32, (LEAF, R), 1).astype(F32)
        for i in range(LEAF // R):
            straight[:, i * R : (i + 1) * R] = jnp.where(
                column == lane + float(i * R), 1.0, 0.0
            ).astype(BF16)

    def fold(which, perm, factor):
        one_hot(perm)

        def fold_rows(i, _):
            at_rows = pl.ds(pl.multiple_of(i * 2 * BLK, 2 * BLK), 2 * BLK)
            got = mm(turned_band[at_rows, which * LEAF : (which + 1) * LEAF], straight[...])
            near_w[which, at_rows, :] = (got * factor).astype(BF16)
            return 0

        lax.fori_loop(0, 2 * LEAF // (2 * BLK), fold_rows, 0)

    def near_part(which, x):
        r = halves(mm(near_w[which], wide(x)))
        return r[:LEAF] + r[LEAF:]

    def pairs(nodes):
        return split(rows(nodes[0::2])) + split(rows(nodes[1::2]))

    def couple(m, pair):
        lh, ll, rh, rl = pair
        to_left = halves(mm(lanes([rh, rl]), coup_w[m, 0]))
        to_right = halves(mm(lanes([lh, ll]), coup_w[m, 1]))
        return to_left, to_right

    def up(m, pair):
        lh, ll, rh, rl = pair
        n = lh.shape[0]
        parent = halves(mm(rows([lanes([lh, rh]), lanes([ll, rl])]), up_w[m]))
        return cut(parent[:n] + parent[n:], n // share)

    def cut(x, parts):
        each = x.shape[0] // parts
        return [x[i * each : (i + 1) * each] for i in range(parts)]

    def down(m, coup, nodes):
        d = halves(mm(wide(rows(nodes)), down_w[m]))
        lefts = cut(coup[0] + d[:, :R], len(nodes))
        rights = cut(coup[1] + d[:, R:], len(nodes))
        return [node for pair in zip(lefts, rights) for node in pair]

    within = log2(team)
    coups = [None] * levels
    all_but_one(up_in, up_recv, team).wait()
    send_halo(3)
    nodes = [up_in[k] for k in range(team)]
    below = []
    for m in range(within):
        below.append(pairs(nodes))
        nodes = up(m, below[m])
    y_out[...] = nodes[0]
    for k in range(1, NY):
        to = lax.rem(y + k, NY)
        remote(y_out, y_in.at[y], y_send, y_recv, y_dev(to)).start()
    y_in[y] = y_out[...]
    for m in range(within - 1, -1, -1):
        coups[m] = couple(m, below[m])
    fold(1, perm_row, 1.0)
    all_but_one(y_in, y_recv, NY).wait()
    nodes = [y_in[k] for k in range(NY)]
    for m in range(within, levels):
        pair = pairs(nodes)
        if m < levels - 1:
            nodes = up(m, pair)
        coups[m] = couple(m, pair)
    nodes = [coups[levels - 1][0], coups[levels - 1][1]]
    for m in range(levels - 2, within - 1, -1):
        nodes = down(m, coups[m], nodes)
    for k in range(NY):
        top[k] = nodes[k]
    nodes = [top[y]]
    for m in range(within - 1, -1, -1):
        nodes = down(m, coups[m], nodes)
    for k in range(team):
        down_out[k] = nodes[k]

    def down_start(k, _):
        to = lax.rem(place + k, team)
        remote(down_out.at[to], down_in.at[place], down_send, down_recv, team_dev(to)).start()
        return 0

    lax.fori_loop(1, team, down_start, 0)
    down_in[place] = down_out[place]

    for side in range(2):
        halo_perm(side).wait_recv()
    fold(0, perm_in[0], jnp.where(leaf > 0, 1.0, 0.0).astype(F32))
    fold(2, perm_in[1], jnp.where(leaf < leaves - 1, 1.0, 0.0).astype(F32))
    for c in range(chunks):
        total[c] = near_part(1, x_v[:, c * CW : (c + 1) * CW])
    for c in range(chunks):
        for side in range(2):
            halo(side, c).wait_recv()
            total[c] = total[c] + near_part(2 * side, raw[side, c])

    all_but_one(down_in, down_recv, team).wait()
    expanded = down_in[...].reshape(NRHS, R)
    for c in range(chunks):
        e = wide(expanded[c * CW : (c + 1) * CW].T)
        product[:, c * CW : (c + 1) * CW] = total[c] + halves(mm(far_w[...], rows([e, e])))
    all_but_one(up_in, up_send, team).wait()
    all_but_one(down_in, down_send, team).wait()
    all_but_one(y_in, y_send, NY).wait()
    for side in range(2):
        halo_perm(side).wait_send()
        for chunk in range(chunks):
            halo(side, chunk).wait_send()


def per_device(
    columns, col_basis, row_basis, order_perm, near_blocks, band_offsets, transfer, coupling
):
    levels = coupling.shape[0]
    chunks = NRHS // CW
    team = NX * NC * NZ
    share = NRHS // team
    transfer = transfer.reshape(levels - 1, 2 * R, R)
    vmem = pltpu.VMEM
    dma = pltpu.SemaphoreType.DMA
    return pl.pallas_call(
        kernel,
        out_shape=vmem((LEAF, NRHS), F32),
        in_specs=[pl.BlockSpec(memory_space=pl.ANY)] * 8,
        out_specs=pl.BlockSpec(memory_space=pltpu.VMEM),
        scratch_shapes=[
            vmem((LEAF, NRHS), F32),
            vmem((LEAF, R), F32),
            vmem((LEAF, R), F32),
            vmem((1, LEAF), jnp.int32),
            vmem((NBLK, NBAND, BLK, BLK), F32),
            pltpu.SMEM((NBLK, NBAND), jnp.int32),
            vmem((levels - 1, 2 * R, R), F32),
            vmem((levels, R, R), F32),
            vmem((levels - 1, 2 * R, 2 * R), BF16),
            vmem((levels - 1, 2 * R, 4 * R), BF16),
            vmem((levels, 2, 2 * R, 2 * R), BF16),
            vmem((2, LEAF, 3 * LEAF), BF16),
            vmem((2 * LEAF, 3 * LEAF), BF16),
            vmem((3, 2 * LEAF, LEAF), BF16),
            vmem((LEAF, 2 * R), BF16),
            vmem((LEAF, LEAF), BF16),
            vmem((LEAF, LEAF), BF16),
            vmem((chunks, LEAF, CW), F32),
            vmem((NRHS, R), F32),
            vmem((team, share, R), F32),
            vmem((share, R), F32),
            vmem((NY, share, R), F32),
            vmem((NY, share, R), F32),
            vmem((team, share, R), F32),
            vmem((team, share, R), F32),
            vmem((2, chunks, LEAF, CW), F32),
            vmem((2, 1, LEAF), jnp.int32),
            dma((8,)),
            dma,
            dma,
            dma,
            dma,
            dma,
            dma,
            dma((2, chunks)),
            dma((2, chunks)),
            dma((2,)),
            dma((2,)),
        ],
        compiler_params=pltpu.CompilerParams(
            collective_id=0, has_side_effects=True, vmem_limit_bytes=58 * 1024 * 1024
        ),
    )(
        columns, col_basis, row_basis, order_perm, near_blocks, band_offsets, transfer, coupling
    )


def solution(mesh):
    placed = (
        P(("gx", "gy"), None),
        P(("gx", "gy"), None),
        P(("gx", "gy"), None),
        P(("gx", "gy"), None),
        P(("gx", "gy"), None, None, None),
        P(("gx", "gy"), None),
        P(),
        P(),
    )
    return jax.shard_map(
        per_device, mesh=mesh, in_specs=placed, out_specs=P(("gx", "gy"), None), check_vma=False
    )
```
